512 devices in a mesh: ctx: 64 (over x, z), tp: 8 (over y, core).
Axes of the slice: x: 4, y: 4, z: 16, core: 2. Of those that a mesh axis runs over, the one named last changes fastest.
Arguments:
- query_in: bfloat16 [12288, 8192], P(('ctx', 'tp')), may hold values from -150 to 150
- key_in: bfloat16 [12288, 1024], P(('ctx', 'tp')), may hold values from -8 to 8
- value_in: bfloat16 [12288, 1024], P(('ctx', 'tp')), may hold values from -6 to 6
- grad_out: bfloat16 [12288, 8192], P(('ctx', 'tp')), may hold values from -24 to 24
- segments: int32 [12288], P('ctx'), may hold values from 0 to 61, as said below
Outputs:
- attn_out: bfloat16 [12288, 8192], P(('ctx', 'tp'))
- grad_query: bfloat16 [12288, 8192], P(('ctx', 'tp'))
- grad_key: bfloat16 [12288, 1024], P(('ctx', 'tp'))
- grad_value: bfloat16 [12288, 1024], P(('ctx', 'tp'))
The draws below stay inside these ranges and needn't reach their ends.
Inputs may be any that keep to these rules, and one draw needn't show every extreme that they name: `segments`: ids start at 0 and never fall along the tokens; each document holds at most 768 tokens, and one holds exactly that many.
All inputs are finite; a program needn't handle non-finite values.
Results may differ from the reference program's by a relative error of at most 0.03.
Values may be sent and summed in bfloat16 or wider, within the bound.
A program may use at most 64 MiB of HBM per device.

```python
import math
import jax
import jax.numpy as jnp
from jax import lax

HEADS = 64
KV_HEADS = 8
HEAD_DIM = 128
TOK_DEV = 192
SPAN = 4
TOKENS = 12288
N_CTX = 64


def shared_draws(key):
    anchor = jax.random.normal(jax.random.fold_in(key, 11), (TOKENS, KV_HEADS, HEAD_DIM), jnp.float32)
    anchor = jnp.clip(anchor, -5.0, 5.0)
    return anchor


def draw_key_in(key, part):
    anchor = shared_draws(key)
    return anchor.reshape(TOKENS, KV_HEADS * HEAD_DIM).astype(jnp.bfloat16)


def draw_query_in(key, part):
    key = jax.random.fold_in(key, 2)
    values = jnp.clip(jax.random.normal(key, (TOKENS, HEADS * HEAD_DIM), jnp.float32), -5.0, 5.0)
    return values.astype(jnp.bfloat16)


def draw_segments(key, part):
    key = jax.random.fold_in(key, 3)
    cut_key, long_key = jax.random.split(key)
    cuts = jax.random.randint(cut_key, (N_CTX,), 1, TOK_DEV, dtype=jnp.int32)
    long_block = jax.random.randint(long_key, (), 1, N_CTX // 2 - SPAN + 1, dtype=jnp.int32)
    block_ids = jnp.arange(N_CTX, dtype=jnp.int32)
    cuts = jnp.where(block_ids == long_block + SPAN, cuts[long_block], cuts)
    positions = jnp.arange(TOKENS, dtype=jnp.int32)
    token_block = positions // TOK_DEV
    token_offset = positions % TOK_DEV
    inner = (token_block > long_block) & (token_block < long_block + SPAN)
    boundary = (token_offset == cuts[token_block]) & jnp.logical_not(inner)
    return jnp.cumsum(boundary.astype(jnp.int32)).astype(jnp.int32)


def shard_levels(own_key, extent, cuts, low, high):
    factor_of, own = 1.0, jax.random.fold_in(own_key, 6)
    for dim, shards_of in cuts:
        steps = jnp.exp(jax.random.uniform(jax.random.fold_in(own, dim), (shards_of,), jnp.float32, low / len(cuts), high / len(cuts)))
        factor_of = factor_of * jnp.repeat(steps, extent[dim] // shards_of).reshape([-1 if axis == dim else 1 for axis in range(len(extent))])
    return factor_of


def scatter_about(key, extent, scale, most, cuts=(), held_as=jnp.bfloat16):
    result = jax.random.normal(key, extent, jnp.float32) * scale
    if len(cuts) > 0:
        result = shard_levels(key, extent, cuts, -0.22, 0.18) * result
    return jnp.clip(result, min=-most, max=most).astype(held_as)


def setup_inputs(seed: int = 0) -> dict:
    streams_of = jax.random.split(jax.random.key(seed), 6)
    return {
        "query_in": draw_query_in(jax.random.fold_in(streams_of[5], 71), 0),
        "key_in": draw_key_in(jax.random.fold_in(streams_of[5], 71), 0),
        "value_in": scatter_about(streams_of[2], (TOKENS, KV_HEADS * HEAD_DIM), 1.0, 6.0, ((0, 512),)),
        "grad_out": scatter_about(streams_of[3], (TOKENS, HEADS * HEAD_DIM), 4.0, 24.0, ((0, 512),)),
        "segments": draw_segments(jax.random.fold_in(streams_of[5], 71), 0),
    }


def reference(query_in, key_in, value_in, grad_out, segments):
    groups = HEADS // KV_HEADS
    window = (SPAN + 1) * TOK_DEV
    scale_factor = 1.0 / math.sqrt(HEAD_DIM)
    positions = jnp.arange(TOKENS, dtype=jnp.int32)
    earlier = jnp.concatenate([jnp.full((1,), -1, jnp.int32), segments[:-1]])
    starts = jnp.where(segments != earlier, positions, jnp.zeros_like(positions))
    doc_first = lax.cummax(starts, axis=0)

    def stretch_step(carried, stretch_index):
        key_grads, value_grads = carried
        query_start = (stretch_index * TOK_DEV).astype(jnp.int32)
        key_start = jnp.clip((stretch_index - SPAN) * TOK_DEV, 0, TOKENS - window).astype(jnp.int32)
        query_block = lax.dynamic_slice_in_dim(query_in, query_start, TOK_DEV, 0).astype(jnp.float32)
        query_block = query_block.reshape(TOK_DEV, KV_HEADS, groups, HEAD_DIM)
        grad_block = lax.dynamic_slice_in_dim(grad_out, query_start, TOK_DEV, 0).astype(jnp.float32)
        grad_block = grad_block.reshape(TOK_DEV, KV_HEADS, groups, HEAD_DIM)
        key_block = lax.dynamic_slice_in_dim(key_in, key_start, window, 0).astype(jnp.float32)
        key_block = key_block.reshape(window, KV_HEADS, HEAD_DIM)
        value_block = lax.dynamic_slice_in_dim(value_in, key_start, window, 0).astype(jnp.float32)
        value_block = value_block.reshape(window, KV_HEADS, HEAD_DIM)
        query_pos = query_start + jnp.arange(TOK_DEV, dtype=jnp.int32)
        key_pos = key_start + jnp.arange(window, dtype=jnp.int32)
        first_block = lax.dynamic_slice_in_dim(doc_first, query_start, TOK_DEV, 0)
        visible = (key_pos[None, :] >= first_block[:, None]) & (key_pos[None, :] <= query_pos[:, None])
        scores = jnp.einsum('tkgd,skd->kgts', query_block, key_block) * scale_factor
        scores = jnp.where(visible[None, None], scores, -jnp.inf)
        row_max = lax.optimization_barrier(jnp.max(scores, axis=-1))
        log_total = row_max + jnp.log(lax.optimization_barrier(jnp.sum(jnp.exp(scores - row_max[..., None]), axis=-1)))
        probs = jnp.exp(scores - log_total[..., None])
        probs_low = lax.optimization_barrier(probs.astype(jnp.bfloat16)).astype(jnp.float32)
        out_block = jnp.einsum('kgts,skd->tkgd', probs_low, value_block).astype(jnp.bfloat16)
        out_wide = lax.optimization_barrier(out_block).astype(jnp.float32)
        row_dot = lax.optimization_barrier(jnp.sum(grad_block * out_wide, axis=-1)).transpose(1, 2, 0)
        dprobs = jnp.einsum('tkgd,skd->kgts', grad_block, value_block)
        dscores = probs * (dprobs - row_dot[..., None])
        dscores = lax.optimization_barrier(dscores.astype(jnp.bfloat16)).astype(jnp.float32)
        query_grad = (jnp.einsum('kgts,skd->tkgd', dscores, key_block) * scale_factor).astype(jnp.bfloat16)
        key_term = jnp.einsum('kgts,tkgd->skd', dscores, query_block) * scale_factor
        value_term = jnp.einsum('kgts,tkgd->skd', probs_low, grad_block)
        old_keys = lax.dynamic_slice_in_dim(key_grads, key_start, window, 0)
        key_grads = lax.dynamic_update_slice_in_dim(key_grads, old_keys + key_term.reshape(window, KV_HEADS * HEAD_DIM), key_start, 0)
        old_values = lax.dynamic_slice_in_dim(value_grads, key_start, window, 0)
        value_grads = lax.dynamic_update_slice_in_dim(value_grads, old_values + value_term.reshape(window, KV_HEADS * HEAD_DIM), key_start, 0)
        return ((key_grads, value_grads), (out_block.reshape(TOK_DEV, HEADS * HEAD_DIM), query_grad.reshape(TOK_DEV, HEADS * HEAD_DIM)))
    start_grads = jnp.zeros((TOKENS, KV_HEADS * HEAD_DIM), jnp.float32)
    (key_grads, value_grads), (out_blocks, query_blocks) = lax.scan(stretch_step, (start_grads, start_grads), jnp.arange(N_CTX, dtype=jnp.int32))
    attn_out = out_blocks.reshape(TOKENS, HEADS * HEAD_DIM)
    grad_query = query_blocks.reshape(TOKENS, HEADS * HEAD_DIM)
    return (attn_out, grad_query, key_grads.astype(jnp.bfloat16), value_grads.astype(jnp.bfloat16))
```

```python
import math

import jax
import jax.numpy as jnp
from jax import lax
from jax.experimental import pallas as pl
from jax.experimental.pallas import tpu as pltpu
from jax.sharding import PartitionSpec as P

HEADS = 64
KV_HEADS = 8
HEAD_DIM = 128
GROUPS = HEADS // KV_HEADS
SPAN = 4
BLOCKS = SPAN + 1
TP = 8
PART = 24
TOK = TP * PART
WIDE = GROUPS * HEAD_DIM
PAIRS = GROUPS // 2
ROWS = 2 * TOK
SCALE = 1.0 / math.sqrt(HEAD_DIM)
SCALE_LOG2 = SCALE * math.log2(math.e)
MASKED = -1e30
MESH = pl.DeviceIdType.MESH
F32 = jnp.float32
BF16 = jnp.bfloat16

NT = (((1,), (1,)), ((), ()))
NN = (((1,), (0,)), ((), ()))


def dot(a, b, dims=NN):
    return lax.dot_general(a, b, dims, preferred_element_type=F32)


def landed(ref, sem):
    pltpu.make_async_copy(ref, ref, sem).wait()


def column_of(row):
    i = lax.broadcasted_iota(jnp.int32, (TOK, TOK), 0)
    j = lax.broadcasted_iota(jnp.int32, (TOK, TOK), 1)
    return jnp.sum(jnp.where(i == j, row, 0.0), axis=1, keepdims=True)


def kernel(
    q_in, k_in, v_in, g_in, seg_in,
    o_out, dq_out, dk_out, dv_out,
    qb, gb, kb, vb,
    kx, vx, sx, vt, kt, bias,
    qp, gp, scores, dprobs, probs, dscores,
    ob, dqb, dkb, dvb,
    tk, tv, rk, rv,
    local_sem, in_send, in_recv, hop_send, hop_recv, back_send, back_recv, out_send, out_recv,
):
    ctx = lax.axis_index("ctx")
    me = lax.axis_index("tp")
    n_ctx = lax.axis_size("ctx")
    after = lax.rem(ctx + 1, n_ctx)
    before = lax.rem(ctx + n_ctx - 1, n_ctx)

    barrier = pltpu.get_barrier_semaphore()

    def greet(j, carry):
        pl.semaphore_signal(
            barrier, inc=1, device_id=(ctx, lax.rem(me + j, TP)), device_id_type=MESH
        )
        return carry

    lax.fori_loop(1, TP, greet, 0)
    pl.semaphore_signal(barrier, inc=1, device_id=(after, me), device_id_type=MESH)
    pl.semaphore_signal(barrier, inc=1, device_id=(before, me), device_id_type=MESH)
    pl.semaphore_wait(barrier, TP + 1)

    def columns(owner, width):
        return pl.ds(pl.multiple_of(owner * width, width), width)

    def scatter(src, buf, width, n):
        def send(j, carry):
            peer = lax.rem(me + j, TP)
            pltpu.make_async_remote_copy(
                src_ref=src.at[:, columns(peer, width)],
                dst_ref=buf.at[me],
                send_sem=in_send.at[n],
                recv_sem=in_recv.at[n],
                device_id=(ctx, peer),
                device_id_type=MESH,
            ).start()
            return carry

        lax.fori_loop(1, TP, send, 0)
        pltpu.make_async_copy(src.at[:, columns(me, width)], buf.at[me], local_sem.at[n]).start()

    def gathered(buf, n):
        landed(buf.at[pl.ds(0, TP - 1)], in_recv.at[n])
        landed(buf.at[0], local_sem.at[n])

    scatter(k_in, kb, HEAD_DIM, 0)
    scatter(v_in, vb, HEAD_DIM, 1)
    scatter(q_in, qb, WIDE, 2)
    scatter(g_in, gb, WIDE, 3)

    def joined(buf, low):
        parts = [buf[r, :, low : low + HEAD_DIM].astype(F32) for r in range(TP)]
        return jnp.concatenate(parts, axis=0).astype(BF16)

    sx[0] = seg_in[...].astype(F32)

    def hop(buf, d, n):
        pltpu.make_async_remote_copy(
            src_ref=buf.at[d],
            dst_ref=buf.at[d + 1],
            send_sem=hop_send.at[n, d],
            recv_sem=hop_recv.at[n, d],
            device_id=(after, me),
            device_id_type=MESH,
        ).start()

    hop(sx, 0, 2)
    gathered(kb, 0)
    kx[0] = joined(kb, 0)
    hop(kx, 0, 0)
    gathered(vb, 1)
    vx[0] = joined(vb, 0)
    hop(vx, 0, 1)
    for d in range(1, BLOCKS):
        for buf, n in ((sx, 2), (kx, 0), (vx, 1)):
            landed(buf.at[d], hop_recv.at[n, d - 1])
            if d < SPAN:
                hop(buf, d, n)

    own = sx[0]
    own_wide = jnp.concatenate([own, own], axis=1)
    for d in range(BLOCKS):
        seen = column_of(sx[d]) == own_wide
        if d == 0:
            i = lax.broadcasted_iota(jnp.int32, (TOK, TOK), 0)
            j = lax.broadcasted_iota(jnp.int32, (TOK, TOK), 1)
            causal = jnp.where(i <= j, 0.0, MASKED)
            bias[d] = jnp.where(seen, jnp.concatenate([causal, causal], axis=1), MASKED)
        else:
            bias[d] = jnp.where(seen, 0.0, MASKED)
        kt[d] = kx[d].astype(F32).T.astype(BF16)
        vt[d] = vx[d].astype(F32).T.astype(BF16)

    gathered(qb, 2)
    for h in range(GROUPS):
        qp[h * TOK : (h + 1) * TOK, :] = joined(qb, h * HEAD_DIM)
    gathered(gb, 3)
    for h in range(GROUPS):
        gp[h * TOK : (h + 1) * TOK, :] = joined(gb, h * HEAD_DIM)

    def pair_step(hp, carry):
        rows = pl.ds(pl.multiple_of(hp * ROWS, ROWS), ROWS)
        q2 = qp[rows, :]
        g2 = gp[rows, :]
        top = None
        for d in range(BLOCKS):
            s = dot(kx[d], q2, NT) * SCALE_LOG2 + bias[d]
            scores[d] = s
            here = jnp.max(s, axis=0, keepdims=True)
            top = here if top is None else jnp.maximum(top, here)
        total = jnp.zeros_like(top)
        weighted = jnp.zeros_like(top)
        for d in range(BLOCKS):
            e = jnp.exp2(scores[d] - top)
            total += jnp.sum(e, axis=0, keepdims=True)
            dp = dot(vx[d], g2, NT)
            weighted += jnp.sum(e * dp, axis=0, keepdims=True)
            scores[d] = e
            dprobs[d] = dp
        inverse = 1.0 / total
        row_dot = weighted * inverse
        o_t = None
        dq_t = None
        for d in range(BLOCKS):
            p = scores[d] * inverse
            p_low = p.astype(BF16)
            ds = (p * (dprobs[d] - row_dot)).astype(BF16)
            probs[d, :, rows] = p_low
            dscores[d, :, rows] = ds
            o_d = dot(vt[d], p_low)
            dq_d = dot(kt[d], ds)
            o_t = o_d if o_t is None else o_t + o_d
            dq_t = dq_d if dq_t is None else dq_t + dq_d
        o = o_t.T
        dq = (dq_t * SCALE).T
        for i in range(2):
            lanes = pl.ds(pl.multiple_of((2 * hp + i) * HEAD_DIM, HEAD_DIM), HEAD_DIM)
            for r in range(TP):
                low = i * TOK + r * PART
                ob[r, :, lanes] = o[low : low + PART].astype(BF16)
                dqb[r, :, lanes] = dq[low : low + PART].astype(BF16)
        return carry

    lax.fori_loop(0, PAIRS, pair_step, 0)

    def give(buf, dst, width, n):
        def send(j, carry):
            peer = lax.rem(me + j, TP)
            pltpu.make_async_remote_copy(
                src_ref=buf.at[peer],
                dst_ref=dst.at[:, columns(me, width)],
                send_sem=out_send.at[n],
                recv_sem=out_recv.at[n],
                device_id=(ctx, peer),
                device_id_type=MESH,
            ).start()
            return carry

        lax.fori_loop(1, TP, send, 0)
        pltpu.make_async_copy(
            buf.at[me], dst.at[:, columns(me, width)], local_sem.at[4 + n]
        ).start()

    def back(src, dst, h, n):
        pltpu.make_async_remote_copy(
            src_ref=src.at[h],
            dst_ref=dst.at[h],
            send_sem=back_send.at[n, h],
            recv_sem=back_recv.at[n, h],
            device_id=(before, me),
            device_id_type=MESH,
        ).start()

    give(ob, o_out, WIDE, 0)
    give(dqb, dq_out, WIDE, 1)

    for h in range(BLOCKS):
        d = SPAN - h
        for n, (left, right, scaling, tx, rx) in enumerate(
            ((probs, gp, 1.0, tv, rv), (dscores, qp, SCALE, tk, rk))
        ):
            term = dot(left[d], right[...]) * scaling
            if h > 0:
                landed(rx.at[h - 1], back_recv.at[n, h - 1])
                term += rx[h - 1].astype(F32)
            if h < SPAN:
                tx[h] = term.astype(BF16)
                back(tx, rx, h, n)
            else:
                final = dvb if n == 0 else dkb
                for r in range(TP):
                    final[r] = term[r * PART : (r + 1) * PART].astype(BF16)
                if n == 0:
                    give(dvb, dv_out, HEAD_DIM, 2)
                else:
                    give(dkb, dk_out, HEAD_DIM, 3)

    for n, (buf, dst) in enumerate(((ob, o_out), (dqb, dq_out), (dvb, dv_out), (dkb, dk_out))):
        landed(buf.at[pl.ds(0, TP - 1)], out_recv.at[n])
        landed(buf.at[0], local_sem.at[4 + n])
        landed(buf.at[pl.ds(0, TP - 1)], out_send.at[n])
    for n, buf in enumerate((kb, vb, qb, gb)):
        landed(buf.at[pl.ds(0, TP - 1)], in_send.at[n])
    for d in range(SPAN):
        for n, buf in enumerate((kx, vx, sx)):
            landed(buf.at[d], hop_send.at[n, d])
        for n, buf in enumerate((tv, tk)):
            landed(buf.at[d], back_send.at[n, d])


def body(query_in, key_in, value_in, grad_out, segments):
    any_spec = pl.BlockSpec(memory_space=pl.ANY)
    vmem_spec = pl.BlockSpec(memory_space=pltpu.VMEM)
    sem = pltpu.SemaphoreType.DMA
    return pl.pallas_call(
        kernel,
        out_shape=(
            jax.ShapeDtypeStruct((PART, HEADS * HEAD_DIM), BF16),
            jax.ShapeDtypeStruct((PART, HEADS * HEAD_DIM), BF16),
            jax.ShapeDtypeStruct((PART, KV_HEADS * HEAD_DIM), BF16),
            jax.ShapeDtypeStruct((PART, KV_HEADS * HEAD_DIM), BF16),
        ),
        in_specs=[any_spec] * 4 + [vmem_spec],
        out_specs=(any_spec,) * 4,
        scratch_shapes=[
            pltpu.VMEM((TP, PART, WIDE), BF16),
            pltpu.VMEM((TP, PART, WIDE), BF16),
            pltpu.VMEM((TP, PART, HEAD_DIM), BF16),
            pltpu.VMEM((TP, PART, HEAD_DIM), BF16),
            pltpu.VMEM((BLOCKS, TOK, HEAD_DIM), BF16),
            pltpu.VMEM((BLOCKS, TOK, HEAD_DIM), BF16),
            pltpu.VMEM((BLOCKS, 1, TOK), F32),
            pltpu.VMEM((BLOCKS, HEAD_DIM, TOK), BF16),
            pltpu.VMEM((BLOCKS, HEAD_DIM, TOK), BF16),
            pltpu.VMEM((BLOCKS, TOK, ROWS), F32),
            pltpu.VMEM((GROUPS * TOK, HEAD_DIM), BF16),
            pltpu.VMEM((GROUPS * TOK, HEAD_DIM), BF16),
            pltpu.VMEM((BLOCKS, TOK, ROWS), F32),
            pltpu.VMEM((BLOCKS, TOK, ROWS), F32),
            pltpu.VMEM((BLOCKS, TOK, GROUPS * TOK), BF16),
            pltpu.VMEM((BLOCKS, TOK, GROUPS * TOK), BF16),
            pltpu.VMEM((TP, PART, WIDE), BF16),
            pltpu.VMEM((TP, PART, WIDE), BF16),
            pltpu.VMEM((TP, PART, HEAD_DIM), BF16),
            pltpu.VMEM((TP, PART, HEAD_DIM), BF16),
            pltpu.VMEM((SPAN, TOK, HEAD_DIM), BF16),
            pltpu.VMEM((SPAN, TOK, HEAD_DIM), BF16),
            pltpu.VMEM((SPAN, TOK, HEAD_DIM), BF16),
            pltpu.VMEM((SPAN, TOK, HEAD_DIM), BF16),
            sem((8,)),
            sem((4,)),
            sem((4,)),
            sem((3, SPAN)),
            sem((3, SPAN)),
            sem((2, SPAN)),
            sem((2, SPAN)),
            sem((4,)),
            sem((4,)),
        ],
        compiler_params=pltpu.CompilerParams(
            collective_id=0, has_side_effects=True, vmem_limit_bytes=48 * 1024 * 1024
        ),
    )(query_in, key_in, value_in, grad_out, segments.reshape(1, TOK))


def solution(mesh):
    split = P(("ctx", "tp"), None)
    return jax.shard_map(
        body,
        mesh=mesh,
        in_specs=(split, split, split, split, P("ctx")),
        out_specs=(split, split, split, split),
        check_vma=False,
    )
```

```python
import math

import jax
import jax.numpy as jnp
from jax import lax
from jax.experimental import pallas as pl
from jax.experimental.pallas import tpu as pltpu
from jax.sharding import PartitionSpec as P

HEADS = 64
KV_HEADS = 8
HEAD_DIM = 128
GROUPS = HEADS // KV_HEADS
SPAN = 4
BLOCKS = SPAN + 1
TP = 8
PART = 24
TOK = TP * PART
WIDE = GROUPS * HEAD_DIM
ALL_ROWS = GROUPS * TOK
PAIR = 2 * TOK
HEAD_ROWS = 16
HALF = TOK // 2
CHUNKS = TP // 2
SCALE = 1.0 / math.sqrt(HEAD_DIM)
SCALE_LOG2 = SCALE * math.log2(math.e)
MASKED = -1e30
MESH = pl.DeviceIdType.MESH
F32 = jnp.float32
BF16 = jnp.bfloat16

NT = (((1,), (1,)), ((), ()))
NN = (((1,), (0,)), ((), ()))

CUTS = ((0, HALF), (HALF, HALF))


def dot(a, b, dims=NN):
    return lax.dot_general(a, b, dims, preferred_element_type=F32)


def landed(ref, sem):
    pltpu.make_async_copy(ref, ref, sem).wait()


def column_of(row):
    i = lax.broadcasted_iota(jnp.int32, (TOK, TOK), 0)
    j = lax.broadcasted_iota(jnp.int32, (TOK, TOK), 1)
    return jnp.sum(jnp.where(i == j, row, 0.0), axis=1, keepdims=True)


def kernel(
    q_in, k_in, v_in, g_in, seg_in,
    o_out, dq_out, dk_out, dv_out,
    qs, gs, ks, vs, qb, gb, kc, vc, sg,
    kx, vx, bias, qp, gp,
    ex, dpx, tops, sums, dots, factors,
    pb, db, terms,
    ob, dqb, near, far, near_in, far_in,
    tx, rx,
    seg_v, load_sem, local_sem, in_send, in_recv, hop_send, hop_recv, back_send, back_recv,
    out_send, out_recv, end_send, end_recv,
):
    ctx = lax.axis_index("ctx")
    me = lax.axis_index("tp")
    n_ctx = lax.axis_size("ctx")
    after = lax.rem(ctx + 1, n_ctx)
    before = lax.rem(ctx + n_ctx - 1, n_ctx)

    loads = [
        pltpu.make_async_copy(src, dst, load_sem.at[n])
        for n, (src, dst) in enumerate(((k_in, ks), (v_in, vs), (q_in, qs), (g_in, gs), (seg_in, seg_v)))
    ]
    for load in loads:
        load.start()

    barrier = pltpu.get_barrier_semaphore()

    def greet(j, carry):
        peer = lax.rem(me + j, TP)
        pl.semaphore_signal(barrier, inc=1, device_id=(after, peer), device_id_type=MESH)
        pl.semaphore_signal(barrier, inc=1, device_id=(before, peer), device_id_type=MESH)
        return carry

    def greet_near(j, carry):
        peer = lax.rem(me + j, TP)
        pl.semaphore_signal(barrier, inc=1, device_id=(ctx, peer), device_id_type=MESH)
        return carry

    lax.fori_loop(0, TP, greet, 0)
    lax.fori_loop(1, TP, greet_near, 0)
    pl.semaphore_wait(barrier, 3 * TP - 1)

    def columns(owner, width):
        return pl.ds(pl.multiple_of(owner * width, width), width)

    def scatter(src, buf, width, n):
        def send(j, carry):
            peer = lax.rem(me + j, TP)
            pltpu.make_async_remote_copy(
                src_ref=src.at[:, columns(peer, width)],
                dst_ref=buf.at[me],
                send_sem=in_send.at[n],
                recv_sem=in_recv.at[n],
                device_id=(ctx, peer),
                device_id_type=MESH,
            ).start()
            return carry

        lax.fori_loop(1, TP, send, 0)
        pltpu.make_async_copy(src.at[:, columns(me, width)], buf.at[me], local_sem.at[n]).start()

    def scatter_on(src, buf, n):
        def send(j, carry):
            peer = lax.rem(me + j, TP)
            pltpu.make_async_remote_copy(
                src_ref=src.at[:, columns(peer, HEAD_DIM)],
                dst_ref=buf.at[1, me],
                send_sem=in_send.at[n],
                recv_sem=in_recv.at[n],
                device_id=(after, peer),
                device_id_type=MESH,
            ).start()
            return carry

        lax.fori_loop(0, TP, send, 0)

    def gathered(buf, n):
        landed(buf.at[pl.ds(0, TP - 1)], in_recv.at[n])
        landed(buf.at[0], local_sem.at[n])

    def joined(buf, low):
        parts = [buf[r, :, low : low + HEAD_DIM].astype(F32) for r in range(TP)]
        return jnp.concatenate(parts, axis=0).astype(BF16)

    def pass_on(src, dst, n, d):
        pltpu.make_async_remote_copy(
            src_ref=src,
            dst_ref=dst,
            send_sem=hop_send.at[n, d],
            recv_sem=hop_recv.at[n, d],
            device_id=(after, me),
            device_id_type=MESH,
        ).start()

    def hop_ids(d):
        if d > 0:
            landed(sg.at[d], hop_recv.at[4, d - 1])
        if d < SPAN:
            pass_on(sg.at[d], sg.at[d + 1], 4, d)

    def hop(buf, d, n):
        if d == 1:
            landed(buf.at[1], in_recv.at[4 + n])
        for c in range(2):
            part = pl.ds(c * CHUNKS, CHUNKS)
            if d > 1:
                landed(buf.at[d, part], hop_recv.at[2 * n + c, d - 1])
            if d < SPAN:
                pass_on(buf.at[d, part], buf.at[d + 1, part], 2 * n + c, d)

    def hop_keys(d):
        hop_ids(d)
        hop(kc, d, 0)

    def hop_values(d):
        hop(vc, d, 1)

    def ids_of(d):
        rows = sg[d].astype(F32)
        return jnp.concatenate([rows[0:1], rows[1:2, : TOK - 128]], axis=1)

    def make_bias(d):
        own = ids_of(0)
        seen = column_of(ids_of(d)) == jnp.concatenate([own, own], axis=1)
        if d == 0:
            i = lax.broadcasted_iota(jnp.int32, (TOK, TOK), 0)
            j = lax.broadcasted_iota(jnp.int32, (TOK, TOK), 1)
            causal = jnp.where(i <= j, 0.0, MASKED)
            bias[d] = jnp.where(seen, jnp.concatenate([causal, causal], axis=1), MASKED)
        else:
            bias[d] = jnp.where(seen, 0.0, MASKED)

    tiles = [slice(c * 128, (c + 1) * 128) for c in range(ALL_ROWS // 128)]
    bias_tiles = [slice((c % 3) * 128, (c % 3 + 1) * 128) for c in range(ALL_ROWS // 128)]

    def keys(d):
        return kx[d]

    def score(d):
        make_bias(d)
        kx[d] = joined(kc.at[d], 0)
        s = dot(keys(d), qp[...], NT)
        for lanes, cover in zip(tiles, bias_tiles):
            x = s[:, lanes] * SCALE_LOG2 + bias[d, :, cover]
            top = jnp.max(x, axis=0, keepdims=True)
            e = jnp.exp2(x - top)
            ex[d, :, lanes] = e
            tops[d, :, lanes] = top
            sums[d, :, lanes] = jnp.sum(e, axis=0, keepdims=True)

    def dprob(d):
        vx[d] = joined(vc.at[d], 0)
        t = dot(vx[d], gp[...], NT)
        for lanes in tiles:
            dp = t[:, lanes]
            dpx[d, :, lanes] = dp
            dots[d, :, lanes] = jnp.sum(ex[d, :, lanes] * dp, axis=0, keepdims=True)

    def combine():
        top = tops[0]
        for d in range(1, BLOCKS):
            top = jnp.maximum(top, tops[d])
        shares = [jnp.exp2(tops[d] - top) for d in range(BLOCKS)]
        inverse = 1.0 / sum(shares[d] * sums[d] for d in range(BLOCKS))
        for d in range(BLOCKS):
            factors[d] = shares[d] * inverse

    def combine_dots():
        factors[BLOCKS] = sum(factors[d] * dots[d] for d in range(BLOCKS))

    def weigh(d):
        for lanes in tiles:
            pb[d, :, lanes] = (ex[d, :, lanes] * factors[d, :, lanes]).astype(BF16)

    def weigh_keys(d):
        for lanes in tiles:
            p = ex[d, :, lanes] * factors[d, :, lanes]
            db[d, :, lanes] = (p * (dpx[d, :, lanes] - factors[BLOCKS, :, lanes])).astype(BF16)

    def value_term(d):
        terms[0, d] = dot(pb[d], gp[...])

    def key_term(d):
        terms[1, d] = dot(db[d], qp[...]) * SCALE

    def back(h, n):
        d = SPAN - h
        for c, (low, size) in enumerate(CUTS):
            rows = pl.ds(low, size)
            term = terms[n, d, rows]
            if h > 0:
                landed(rx.at[n, h - 1, rows], back_recv.at[2 * n + c, h - 1])
                term += rx[n, h - 1, rows].astype(F32)
            if h < SPAN - 1:
                tx[n, h, rows] = term.astype(BF16)
                pltpu.make_async_remote_copy(
                    src_ref=tx.at[n, h, rows],
                    dst_ref=rx.at[n, h, rows],
                    send_sem=back_send.at[2 * n + c, h],
                    recv_sem=back_recv.at[2 * n + c, h],
                    device_id=(before, me),
                    device_id_type=MESH,
                ).start()
            else:
                for r in range(CHUNKS):
                    far[n, c * CHUNKS + r] = term[r * PART : (r + 1) * PART].astype(BF16)

                def send(j, carry):
                    pltpu.make_async_remote_copy(
                        src_ref=far.at[n, j],
                        dst_ref=far_in.at[n, me],
                        send_sem=end_send.at[n],
                        recv_sem=end_recv.at[n],
                        device_id=(before, j),
                        device_id_type=MESH,
                    ).start()
                    return carry

                lax.fori_loop(c * CHUNKS, (c + 1) * CHUNKS, send, 0)

    def own_terms(n):
        for r in range(TP):
            near[n, r] = terms[n, 0, r * PART : (r + 1) * PART].astype(BF16)

        def send(j, carry):
            peer = lax.rem(me + j, TP)
            pltpu.make_async_remote_copy(
                src_ref=near.at[n, peer],
                dst_ref=near_in.at[n, me],
                send_sem=out_send.at[2 + n],
                recv_sem=out_recv.at[2 + n],
                device_id=(ctx, peer),
                device_id_type=MESH,
            ).start()
            return carry

        lax.fori_loop(1, TP, send, 0)
        pltpu.make_async_copy(near.at[n, me], near_in.at[n, me], local_sem.at[6 + n]).start()

    def close(n, dst):
        landed(near_in.at[n, pl.ds(0, TP - 1)], out_recv.at[2 + n])
        landed(near_in.at[n, 0], local_sem.at[6 + n])
        landed(far_in.at[n], end_recv.at[n])
        for h in range(TP):
            total = near_in[n, h].astype(F32) + far_in[n, h].astype(F32)
            dst[:, h * HEAD_DIM : (h + 1) * HEAD_DIM] = total.astype(BF16)

    def give(buf, dst, width, n):
        def send(j, carry):
            peer = lax.rem(me + j, TP)
            pltpu.make_async_remote_copy(
                src_ref=buf.at[peer],
                dst_ref=dst.at[:, columns(me, width)],
                send_sem=out_send.at[n],
                recv_sem=out_recv.at[n],
                device_id=(ctx, peer),
                device_id_type=MESH,
            ).start()
            return carry

        lax.fori_loop(1, TP, send, 0)
        pltpu.make_async_copy(
            buf.at[me], dst.at[:, columns(me, width)], local_sem.at[4 + n]
        ).start()

    def product(parts, low, scaling, buf, dst, n):
        for h in range(0, GROUPS, 2):
            lanes = slice(h * TOK, h * TOK + PAIR)
            total = None
            for d in range(BLOCKS):
                one = dot(low(d), parts[d, :, lanes])
                total = one if total is None else total + one
            both = (total * scaling).T
            for i in range(2):
                for r in range(TP):
                    start = i * TOK + r * PART
                    buf[r, :, (h + i) * HEAD_DIM : (h + i + 1) * HEAD_DIM] = both[
                        start : start + PART
                    ].astype(BF16)
        give(buf, dst, WIDE, n)

    def drain():
        for n, (buf, dst) in enumerate(((ob, o_out), (dqb, dq_out))):
            landed(buf.at[pl.ds(0, TP - 1)], out_recv.at[n])
            landed(buf.at[0], local_sem.at[4 + n])
            landed(buf.at[pl.ds(0, TP - 1)], out_send.at[n])
        for n, buf in enumerate((kc.at[0], vc.at[0], qb, gb)):
            landed(buf.at[pl.ds(0, TP - 1)], in_send.at[n])
        for n, buf in enumerate((kc, vc)):
            landed(buf.at[1], in_send.at[4 + n])
        landed(sg.at[0], hop_send.at[4, 0])
        for d in range(1, SPAN):
            landed(sg.at[d], hop_send.at[4, d])
            for c in range(2):
                part = pl.ds(c * CHUNKS, CHUNKS)
                landed(kc.at[d, part], hop_send.at[c, d])
                landed(vc.at[d, part], hop_send.at[2 + c, d])
        for n in range(2):
            for h in range(SPAN - 1):
                for c, (low, size) in enumerate(CUTS):
                    landed(tx.at[n, h, pl.ds(low, size)], back_send.at[2 * n + c, h])
            landed(near.at[n, pl.ds(0, TP - 1)], out_send.at[2 + n])
            landed(far.at[n], end_send.at[n])

    loads[4].wait()
    ids = seg_v[...].astype(F32)
    late_ids = jnp.concatenate([ids[:, 128:TOK], jnp.zeros((1, 256 - TOK), F32)], axis=1)
    place = lax.broadcasted_iota(jnp.int32, (HEAD_ROWS, 128), 0)
    head = jnp.where(place == 0, ids[:, :128], jnp.where(place == 1, late_ids, 0.0))
    sg[0] = head.astype(BF16)
    loads[0].wait()
    loads[1].wait()
    scatter_on(ks, kc, 4)
    hop_ids(0)
    scatter(ks, kc.at[0], HEAD_DIM, 0)
    scatter_on(vs, vc, 5)
    scatter(vs, vc.at[0], HEAD_DIM, 1)
    loads[2].wait()
    scatter(qs, qb, WIDE, 2)
    hop_keys(1)
    hop_values(1)
    loads[3].wait()
    scatter(gs, gb, WIDE, 3)
    hop_keys(2)
    hop_values(2)
    gathered(qb, 2)
    for h in range(GROUPS):
        qp[h * TOK : (h + 1) * TOK, :] = joined(qb, h * HEAD_DIM)
    gathered(kc.at[0], 0)
    score(0)
    hop_keys(3)
    score(1)
    hop_values(3)
    score(2)
    score(3)
    gathered(gb, 3)
    for h in range(GROUPS):
        gp[h * TOK : (h + 1) * TOK, :] = joined(gb, h * HEAD_DIM)
    gathered(vc.at[0], 1)
    dprob(0)
    dprob(1)
    dprob(2)
    dprob(3)
    hop_keys(4)
    score(4)
    combine()
    weigh(4)
    value_term(4)
    back(0, 0)
    weigh(3)
    weigh(2)
    hop_values(4)
    dprob(4)
    combine_dots()
    weigh_keys(4)
    key_term(4)
    back(0, 1)
    weigh(1)
    weigh(0)
    product(pb, lambda d: vx[d].astype(F32).T.astype(BF16), 1.0, ob, o_out, 0)
    value_term(3)
    back(1, 0)
    weigh_keys(3)
    key_term(3)
    back(1, 1)
    weigh_keys(2)
    weigh_keys(1)
    weigh_keys(0)
    product(db, lambda d: keys(d).astype(F32).T.astype(BF16), SCALE, dqb, dq_out, 1)
    value_term(2)
    back(2, 0)
    key_term(2)
    back(2, 1)
    value_term(0)
    own_terms(0)
    key_term(0)
    own_terms(1)
    value_term(1)
    back(3, 0)
    key_term(1)
    back(3, 1)
    close(0, dv_out)
    close(1, dk_out)
    drain()


def deliver(o, dq, dk, dv, o_out, dq_out, dk_out, dv_out, sems):
    copies = [
        pltpu.make_async_copy(src, dst, sems.at[n])
        for n, (src, dst) in enumerate(((o, o_out), (dq, dq_out), (dk, dk_out), (dv, dv_out)))
    ]
    for copy in copies:
        copy.start()
    for copy in copies:
        copy.wait()


def body(query_in, key_in, value_in, grad_out, segments):
    hbm_spec = pl.BlockSpec(memory_space=pltpu.HBM)
    vmem_spec = pl.BlockSpec(memory_space=pltpu.VMEM)
    sem = pltpu.SemaphoreType.DMA
    outs = (
        jax.ShapeDtypeStruct((PART, HEADS * HEAD_DIM), BF16),
        jax.ShapeDtypeStruct((PART, HEADS * HEAD_DIM), BF16),
        jax.ShapeDtypeStruct((PART, KV_HEADS * HEAD_DIM), BF16),
        jax.ShapeDtypeStruct((PART, KV_HEADS * HEAD_DIM), BF16),
    )
    results = pl.pallas_call(
        kernel,
        out_shape=outs,
        in_specs=[hbm_spec] * 5,
        out_specs=(vmem_spec,) * 4,
        scratch_shapes=[
            pltpu.VMEM((PART, HEADS * HEAD_DIM), BF16),
            pltpu.VMEM((PART, HEADS * HEAD_DIM), BF16),
            pltpu.VMEM((PART, KV_HEADS * HEAD_DIM), BF16),
            pltpu.VMEM((PART, KV_HEADS * HEAD_DIM), BF16),
            pltpu.VMEM((TP, PART, WIDE), BF16),
            pltpu.VMEM((TP, PART, WIDE), BF16),
            pltpu.VMEM((BLOCKS, TP, PART, HEAD_DIM), BF16),
            pltpu.VMEM((BLOCKS, TP, PART, HEAD_DIM), BF16),
            pltpu.VMEM((BLOCKS, HEAD_ROWS, 128), BF16),
            pltpu.VMEM((BLOCKS, TOK, HEAD_DIM), BF16),
            pltpu.VMEM((BLOCKS, TOK, HEAD_DIM), BF16),
            pltpu.VMEM((BLOCKS, TOK, PAIR), F32),
            pltpu.VMEM((ALL_ROWS, HEAD_DIM), BF16),
            pltpu.VMEM((ALL_ROWS, HEAD_DIM), BF16),
            pltpu.VMEM((BLOCKS, TOK, ALL_ROWS), F32),
            pltpu.VMEM((BLOCKS, TOK, ALL_ROWS), F32),
            pltpu.VMEM((BLOCKS, 1, ALL_ROWS), F32),
            pltpu.VMEM((BLOCKS, 1, ALL_ROWS), F32),
            pltpu.VMEM((BLOCKS, 1, ALL_ROWS), F32),
            pltpu.VMEM((BLOCKS + 1, 1, ALL_ROWS), F32),
            pltpu.VMEM((BLOCKS, TOK, ALL_ROWS), BF16),
            pltpu.VMEM((BLOCKS, TOK, ALL_ROWS), BF16),
            pltpu.VMEM((2, BLOCKS, TOK, HEAD_DIM), F32),
            pltpu.VMEM((TP, PART, WIDE), BF16),
            pltpu.VMEM((TP, PART, WIDE), BF16),
            pltpu.VMEM((2, TP, PART, HEAD_DIM), BF16),
            pltpu.VMEM((2, TP, PART, HEAD_DIM), BF16),
            pltpu.VMEM((2, TP, PART, HEAD_DIM), BF16),
            pltpu.VMEM((2, TP, PART, HEAD_DIM), BF16),
            pltpu.VMEM((2, SPAN - 1, TOK, HEAD_DIM), BF16),
            pltpu.VMEM((2, SPAN - 1, TOK, HEAD_DIM), BF16),
            pltpu.VMEM((1, TOK), jnp.int32),
            sem((5,)),
            sem((8,)),
            sem((6,)),
            sem((6,)),
            sem((5, SPAN)),
            sem((5, SPAN)),
            sem((4, SPAN - 1)),
            sem((4, SPAN - 1)),
            sem((4,)),
            sem((4,)),
            sem((2,)),
            sem((2,)),
        ],
        compiler_params=pltpu.CompilerParams(
            collective_id=0, has_side_effects=True, vmem_limit_bytes=62 * 1024 * 1024
        ),
    )(query_in, key_in, value_in, grad_out, segments.reshape(1, TOK))
    return pl.pallas_call(
        deliver,
        out_shape=outs,
        in_specs=[vmem_spec] * 4,
        out_specs=(hbm_spec,) * 4,
        scratch_shapes=[sem((4,))],
    )(*results)


def solution(mesh):
    split = P(("ctx", "tp"), None)
    return jax.shard_map(
        body,
        mesh=mesh,
        in_specs=(split, split, split, split, P("ctx")),
        out_specs=(split, split, split, split),
        check_vma=False,
    )
```

```python
import math

import jax
import jax.numpy as jnp
from jax import lax
from jax.experimental import pallas as pl
from jax.experimental.pallas import tpu as pltpu
from jax.sharding import PartitionSpec as P

HEADS = 64
KV_HEADS = 8
HEAD_DIM = 128
GROUPS = HEADS // KV_HEADS
SPAN = 4
BLOCKS = SPAN + 1
TP = 8
PART = 24
TOK = TP * PART
WIDE = GROUPS * HEAD_DIM
ALL_ROWS = GROUPS * TOK
PAIR = 2 * TOK
HEAD_ROWS = 16
HALF = TOK // 2
CHUNKS = TP // 2
SCALE = 1.0 / math.sqrt(HEAD_DIM)
SCALE_LOG2 = SCALE * math.log2(math.e)
MASKED = -1e30
MESH = pl.DeviceIdType.MESH
F32 = jnp.float32
BF16 = jnp.bfloat16

NT = (((1,), (1,)), ((), ()))
NN = (((1,), (0,)), ((), ()))

CUTS = ((0, HALF), (HALF, HALF))


def dot(a, b, dims=NN):
    return lax.dot_general(a, b, dims, preferred_element_type=F32)


def landed(ref, sem):
    pltpu.make_async_copy(ref, ref, sem).wait()


def column_of(row):
    i = lax.broadcasted_iota(jnp.int32, (TOK, TOK), 0)
    j = lax.broadcasted_iota(jnp.int32, (TOK, TOK), 1)
    return jnp.sum(jnp.where(i == j, row, 0.0), axis=1, keepdims=True)


def kernel(
    q_in, k_in, v_in, g_in, seg_in,
    o_out, dq_out, dk_out, dv_out,
    qs, gs, ks, vs, qb, gb, kc, vc, sg,
    kx, vx, bias, qp, gp,
    ex, dpx, tops, sums, dots, factors,
    pb, db, terms,
    ob, dqb, near, far, near_in, far_in,
    tx, rx,
    seg_v, load_sem, local_sem, in_send, in_recv, hop_send, hop_recv, back_send, back_recv,
    out_send, out_recv, end_send, end_recv, present,
):
    ctx = lax.axis_index("ctx")
    me = lax.axis_index("tp")
    n_ctx = lax.axis_size("ctx")
    after = lax.rem(ctx + 1, n_ctx)
    before = lax.rem(ctx + n_ctx - 1, n_ctx)

    loads = [
        pltpu.make_async_copy(src, dst, load_sem.at[n])
        for n, (src, dst) in enumerate(((k_in, ks), (v_in, vs), (q_in, qs), (g_in, gs), (seg_in, seg_v)))
    ]
    for load in loads:
        load.start()

    barrier = pltpu.get_barrier_semaphore()

    def greet(j, carry):
        peer = lax.rem(me + TP // 2 + j, TP)
        pl.semaphore_signal(barrier, inc=1, device_id=(before, peer), device_id_type=MESH)
        return carry

    def greet_on(j, carry):
        peer = lax.rem(me + j, TP)
        pl.semaphore_signal(present, inc=1, device_id=(after, peer), device_id_type=MESH)
        return carry

    def greet_near(j, carry):
        peer = lax.rem(me + j, TP)
        pl.semaphore_signal(barrier, inc=1, device_id=(ctx, peer), device_id_type=MESH)
        return carry

    lax.fori_loop(0, TP, greet, 0)
    lax.fori_loop(1, TP, greet_near, 0)
    pl.semaphore_wait(barrier, 2 * TP - 1)

    def columns(owner, width):
        return pl.ds(pl.multiple_of(owner * width, width), width)

    def scatter(src, buf, width, n):
        def send(j, carry):
            peer = lax.rem(me + j, TP)
            pltpu.make_async_remote_copy(
                src_ref=src.at[:, columns(peer, width)],
                dst_ref=buf.at[me],
                send_sem=in_send.at[n],
                recv_sem=in_recv.at[n],
                device_id=(ctx, peer),
                device_id_type=MESH,
            ).start()
            return carry

        lax.fori_loop(1, TP, send, 0)
        pltpu.make_async_copy(src.at[:, columns(me, width)], buf.at[me], local_sem.at[n]).start()

    def scatter_on(src, buf, n):
        def send(j, carry):
            peer = lax.rem(me + TP // 2 + j, TP)
            pltpu.make_async_remote_copy(
                src_ref=src.at[:, columns(peer, HEAD_DIM)],
                dst_ref=buf.at[1, me],
                send_sem=in_send.at[n],
                recv_sem=in_recv.at[n],
                device_id=(after, peer),
                device_id_type=MESH,
            ).start()
            return carry

        lax.fori_loop(0, TP, send, 0)

    def gathered(buf, n):
        landed(buf.at[pl.ds(0, TP - 1)], in_recv.at[n])
        landed(buf.at[0], local_sem.at[n])

    def joined(buf, low):
        parts = [buf[r, :, low : low + HEAD_DIM].astype(F32) for r in range(TP)]
        return jnp.concatenate(parts, axis=0).astype(BF16)

    def pass_on(src, dst, n, d):
        pltpu.make_async_remote_copy(
            src_ref=src,
            dst_ref=dst,
            send_sem=hop_send.at[n, d],
            recv_sem=hop_recv.at[n, d],
            device_id=(after, me),
            device_id_type=MESH,
        ).start()

    def hop_ids(d):
        if d > 0:
            landed(sg.at[d], hop_recv.at[4, d - 1])
        if d < SPAN:
            pass_on(sg.at[d], sg.at[d + 1], 4, d)

    def hop(buf, d, n):
        if d == 1:
            landed(buf.at[1], in_recv.at[4 + n])
        for c in range(2):
            part = pl.ds(c * CHUNKS, CHUNKS)
            if d > 1:
                landed(buf.at[d, part], hop_recv.at[2 * n + c, d - 1])
            if d < SPAN:
                pass_on(buf.at[d, part], buf.at[d + 1, part], 2 * n + c, d)

    def hop_keys(d):
        hop(kc, d, 0)

    def hop_values(d):
        hop(vc, d, 1)

    def ids_of(d):
        rows = sg[d].astype(F32)
        return jnp.concatenate([rows[0:1], rows[1:2, : TOK - 128]], axis=1)

    def make_bias(d):
        own = ids_of(0)
        seen = column_of(ids_of(d)) == jnp.concatenate([own, own], axis=1)
        if d == 0:
            i = lax.broadcasted_iota(jnp.int32, (TOK, TOK), 0)
            j = lax.broadcasted_iota(jnp.int32, (TOK, TOK), 1)
            causal = jnp.where(i <= j, 0.0, MASKED)
            bias[d] = jnp.where(seen, jnp.concatenate([causal, causal], axis=1), MASKED)
        else:
            bias[d] = jnp.where(seen, 0.0, MASKED)

    tiles = [slice(c * 128, (c + 1) * 128) for c in range(ALL_ROWS // 128)]
    bias_tiles = [slice((c % 3) * 128, (c % 3 + 1) * 128) for c in range(ALL_ROWS // 128)]

    def keys(d):
        return kx[d]

    def score(d):
        kx[d] = joined(kc.at[d], 0)
        s = dot(keys(d), qp[...], NT)
        for lanes, cover in zip(tiles, bias_tiles):
            x = s[:, lanes] * SCALE_LOG2 + bias[d, :, cover]
            top = jnp.max(x, axis=0, keepdims=True)
            e = jnp.exp2(x - top)
            ex[d, :, lanes] = e
            tops[d, :, lanes] = top
            sums[d, :, lanes] = jnp.sum(e, axis=0, keepdims=True)

    def take_values(d):
        vx[d] = joined(vc.at[d], 0)

    def dprob(d):
        t = dot(vx[d], gp[...], NT)
        for lanes in tiles:
            dp = t[:, lanes]
            dpx[d, :, lanes] = dp
            dots[d, :, lanes] = jnp.sum(ex[d, :, lanes] * dp, axis=0, keepdims=True)

    def combine():
        top = tops[0]
        for d in range(1, BLOCKS):
            top = jnp.maximum(top, tops[d])
        shares = [jnp.exp2(tops[d] - top) for d in range(BLOCKS)]
        inverse = 1.0 / sum(shares[d] * sums[d] for d in range(BLOCKS))
        for d in range(BLOCKS):
            factors[d] = shares[d] * inverse

    def combine_dots():
        factors[BLOCKS] = sum(factors[d] * dots[d] for d in range(BLOCKS))

    def weigh(d):
        for lanes in tiles:
            pb[d, :, lanes] = (ex[d, :, lanes] * factors[d, :, lanes]).astype(BF16)

    def weigh_keys(d):
        for lanes in tiles:
            p = ex[d, :, lanes] * factors[d, :, lanes]
            db[d, :, lanes] = (p * (dpx[d, :, lanes] - factors[BLOCKS, :, lanes])).astype(BF16)

    def value_term(d):
        terms[0, d] = dot(pb[d], gp[...])

    def key_term(d):
        terms[1, d] = dot(db[d], qp[...]) * SCALE

    def back(h, n):
        d = SPAN - h
        for c, (low, size) in enumerate(CUTS):
            rows = pl.ds(low, size)
            term = terms[n, d, rows]
            if h > 0:
                landed(rx.at[n, h - 1, rows], back_recv.at[2 * n + c, h - 1])
                term += rx[n, h - 1, rows].astype(F32)
            if h < SPAN - 1:
                tx[n, h, rows] = term.astype(BF16)
                pltpu.make_async_remote_copy(
                    src_ref=tx.at[n, h, rows],
                    dst_ref=rx.at[n, h, rows],
                    send_sem=back_send.at[2 * n + c, h],
                    recv_sem=back_recv.at[2 * n + c, h],
                    device_id=(before, me),
                    device_id_type=MESH,
                ).start()
            else:
                for r in range(CHUNKS):
                    far[n, c * CHUNKS + r] = term[r * PART : (r + 1) * PART].astype(BF16)

                def send(j, carry):
                    pltpu.make_async_remote_copy(
                        src_ref=far.at[n, j],
                        dst_ref=far_in.at[n, me],
                        send_sem=end_send.at[n],
                        recv_sem=end_recv.at[n],
                        device_id=(before, j),
                        device_id_type=MESH,
                    ).start()
                    return carry

                lax.fori_loop(c * CHUNKS, (c + 1) * CHUNKS, send, 0)

    def own_terms(n):
        for r in range(TP):
            near[n, r] = terms[n, 0, r * PART : (r + 1) * PART].astype(BF16)

        def send(j, carry):
            peer = lax.rem(me + j, TP)
            pltpu.make_async_remote_copy(
                src_ref=near.at[n, peer],
                dst_ref=near_in.at[n, me],
                send_sem=out_send.at[2 + n],
                recv_sem=out_recv.at[2 + n],
                device_id=(ctx, peer),
                device_id_type=MESH,
            ).start()
            return carry

        lax.fori_loop(1, TP, send, 0)
        pltpu.make_async_copy(near.at[n, me], near_in.at[n, me], local_sem.at[6 + n]).start()

    def close(n, dst):
        landed(near_in.at[n, pl.ds(0, TP - 1)], out_recv.at[2 + n])
        landed(near_in.at[n, 0], local_sem.at[6 + n])
        landed(far_in.at[n], end_recv.at[n])
        for h in range(TP):
            total = near_in[n, h].astype(F32) + far_in[n, h].astype(F32)
            dst[:, h * HEAD_DIM : (h + 1) * HEAD_DIM] = total.astype(BF16)

    def product(parts, low, scaling, buf, dst, n, cuts):
        turned = [low(d).astype(F32).T.astype(BF16) for d in range(BLOCKS)]
        for cut in range(cuts):
            for h in range(cut * GROUPS // cuts, (cut + 1) * GROUPS // cuts, 2):
                lanes = slice(h * TOK, h * TOK + PAIR)
                total = sum(dot(turned[d], parts[d, :, lanes]) for d in range(BLOCKS))
                both = (total * scaling).T
                for i in range(2):
                    for r in range(TP):
                        start = i * TOK + r * PART
                        buf[r, :, (h + i) * HEAD_DIM : (h + i + 1) * HEAD_DIM] = both[
                            start : start + PART
                        ].astype(BF16)
            size = WIDE // cuts

            def send(j, carry, cut=cut, size=size):
                peer = lax.rem(me + j, TP)
                lanes = pl.ds(pl.multiple_of(me * WIDE + cut * size, HEAD_DIM), size)
                pltpu.make_async_remote_copy(
                    src_ref=buf.at[peer, :, pl.ds(cut * size, size)],
                    dst_ref=dst.at[:, lanes],
                    send_sem=out_send.at[n],
                    recv_sem=out_recv.at[n],
                    device_id=(ctx, peer),
                    device_id_type=MESH,
                ).start()
                return carry

            lax.fori_loop(1, TP, send, 0)
        pltpu.make_async_copy(buf.at[me], dst.at[:, columns(me, WIDE)], local_sem.at[4 + n]).start()

    def drain():
        for n, (buf, dst) in enumerate(((ob, o_out), (dqb, dq_out))):
            landed(buf.at[pl.ds(0, TP - 1)], out_recv.at[n])
            landed(buf.at[0], local_sem.at[4 + n])
            landed(buf.at[pl.ds(0, TP - 1)], out_send.at[n])
        for n, buf in enumerate((kc.at[0], vc.at[0], qb, gb)):
            landed(buf.at[pl.ds(0, TP - 1)], in_send.at[n])
        for n, buf in enumerate((kc, vc)):
            landed(buf.at[1], in_send.at[4 + n])
        landed(sg.at[0], hop_send.at[4, 0])
        for d in range(1, SPAN):
            landed(sg.at[d], hop_send.at[4, d])
            for c in range(2):
                part = pl.ds(c * CHUNKS, CHUNKS)
                landed(kc.at[d, part], hop_send.at[c, d])
                landed(vc.at[d, part], hop_send.at[2 + c, d])
        for n in range(2):
            for h in range(SPAN - 1):
                for c, (low, size) in enumerate(CUTS):
                    landed(tx.at[n, h, pl.ds(low, size)], back_send.at[2 * n + c, h])
            landed(near.at[n, pl.ds(0, TP - 1)], out_send.at[2 + n])
            landed(far.at[n], end_send.at[n])

    loads[4].wait()
    ids = seg_v[...].astype(F32)
    late_ids = jnp.concatenate([ids[:, 128:TOK], jnp.zeros((1, 256 - TOK), F32)], axis=1)
    place = lax.broadcasted_iota(jnp.int32, (HEAD_ROWS, 128), 0)
    head = jnp.where(place == 0, ids[:, :128], jnp.where(place == 1, late_ids, 0.0))
    sg[0] = head.astype(BF16)
    loads[0].wait()
    scatter_on(ks, kc, 4)
    hop_ids(0)
    scatter(ks, kc.at[0], HEAD_DIM, 0)
    loads[1].wait()
    scatter_on(vs, vc, 5)
    scatter(vs, vc.at[0], HEAD_DIM, 1)
    loads[2].wait()
    scatter(qs, qb, WIDE, 2)
    lax.fori_loop(0, TP, greet_on, 0)
    hop_ids(1)
    hop_keys(1)
    hop_values(1)
    loads[3].wait()
    scatter(gs, gb, WIDE, 3)
    make_bias(0)
    make_bias(1)
    hop_ids(2)
    hop_keys(2)
    hop_values(2)
    gathered(qb, 2)
    for h in range(GROUPS):
        qp[h * TOK : (h + 1) * TOK, :] = joined(qb, h * HEAD_DIM)
    gathered(kc.at[0], 0)
    score(0)
    hop_ids(3)
    hop_keys(3)
    score(1)
    hop_values(3)
    make_bias(2)
    score(2)
    make_bias(3)
    score(3)
    hop_ids(4)
    make_bias(4)
    gathered(gb, 3)
    for h in range(GROUPS):
        gp[h * TOK : (h + 1) * TOK, :] = joined(gb, h * HEAD_DIM)
    gathered(vc.at[0], 1)
    take_values(0)
    dprob(0)
    take_values(1)
    dprob(1)
    take_values(2)
    dprob(2)
    take_values(3)
    dprob(3)
    hop_keys(4)
    score(4)
    combine()
    weigh(4)
    value_term(4)
    pl.semaphore_wait(present, TP)
    back(0, 0)
    for d in range(SPAN):
        weigh(d)
    hop_values(4)
    take_values(4)
    dprob(4)
    combine_dots()
    product(pb, lambda d: vx[d], 1.0, ob, o_out, 0, 2)
    weigh_keys(4)
    key_term(4)
    back(0, 1)
    for d in range(SPAN):
        weigh_keys(d)
    product(db, lambda d: keys(d), SCALE, dqb, dq_out, 1, 2)
    value_term(3)
    back(1, 0)
    key_term(3)
    back(1, 1)
    value_term(2)
    back(2, 0)
    key_term(2)
    back(2, 1)
    value_term(0)
    own_terms(0)
    key_term(0)
    own_terms(1)
    value_term(1)
    back(3, 0)
    key_term(1)
    back(3, 1)
    close(0, dv_out)
    close(1, dk_out)
    drain()


def deliver(o, dq, dk, dv, o_out, dq_out, dk_out, dv_out, ov, dqv, dkv, dvv, in_sems, out_sems):
    rows = ((o, ov, o_out), (dq, dqv, dq_out), (dk, dkv, dk_out), (dv, dvv, dv_out))
    fetches = [pltpu.make_async_copy(a, b, in_sems.at[n]) for n, (a, b, _) in enumerate(rows)]
    writes = [pltpu.make_async_copy(b, c, out_sems.at[n]) for n, (_, b, c) in enumerate(rows)]
    for fetch in fetches:
        fetch.start()
    for fetch, write in zip(fetches, writes):
        fetch.wait()
        write.start()
    for write in writes:
        write.wait()


def body(query_in, key_in, value_in, grad_out, segments):
    hbm_spec = pl.BlockSpec(memory_space=pltpu.HBM)
    vmem_spec = pl.BlockSpec(memory_space=pltpu.VMEM)
    sem = pltpu.SemaphoreType.DMA
    outs = (
        jax.ShapeDtypeStruct((PART, HEADS * HEAD_DIM), BF16),
        jax.ShapeDtypeStruct((PART, HEADS * HEAD_DIM), BF16),
        jax.ShapeDtypeStruct((PART, KV_HEADS * HEAD_DIM), BF16),
        jax.ShapeDtypeStruct((PART, KV_HEADS * HEAD_DIM), BF16),
    )
    results = pl.pallas_call(
        kernel,
        out_shape=outs,
        in_specs=[hbm_spec] * 5,
        out_specs=(vmem_spec,) * 4,
        scratch_shapes=[
            pltpu.VMEM((PART, HEADS * HEAD_DIM), BF16),
            pltpu.VMEM((PART, HEADS * HEAD_DIM), BF16),
            pltpu.VMEM((PART, KV_HEADS * HEAD_DIM), BF16),
            pltpu.VMEM((PART, KV_HEADS * HEAD_DIM), BF16),
            pltpu.VMEM((TP, PART, WIDE), BF16),
            pltpu.VMEM((TP, PART, WIDE), BF16),
            pltpu.VMEM((BLOCKS, TP, PART, HEAD_DIM), BF16),
            pltpu.VMEM((BLOCKS, TP, PART, HEAD_DIM), BF16),
            pltpu.VMEM((BLOCKS, HEAD_ROWS, 128), BF16),
            pltpu.VMEM((BLOCKS, TOK, HEAD_DIM), BF16),
            pltpu.VMEM((BLOCKS, TOK, HEAD_DIM), BF16),
            pltpu.VMEM((BLOCKS, TOK, PAIR), F32),
            pltpu.VMEM((ALL_ROWS, HEAD_DIM), BF16),
            pltpu.VMEM((ALL_ROWS, HEAD_DIM), BF16),
            pltpu.VMEM((BLOCKS, TOK, ALL_ROWS), F32),
            pltpu.VMEM((BLOCKS, TOK, ALL_ROWS), F32),
            pltpu.VMEM((BLOCKS, 1, ALL_ROWS), F32),
            pltpu.VMEM((BLOCKS, 1, ALL_ROWS), F32),
            pltpu.VMEM((BLOCKS, 1, ALL_ROWS), F32),
            pltpu.VMEM((BLOCKS + 1, 1, ALL_ROWS), F32),
            pltpu.VMEM((BLOCKS, TOK, ALL_ROWS), BF16),
            pltpu.VMEM((BLOCKS, TOK, ALL_ROWS), BF16),
            pltpu.VMEM((2, BLOCKS, TOK, HEAD_DIM), F32),
            pltpu.VMEM((TP, PART, WIDE), BF16),
            pltpu.VMEM((TP, PART, WIDE), BF16),
            pltpu.VMEM((2, TP, PART, HEAD_DIM), BF16),
            pltpu.VMEM((2, TP, PART, HEAD_DIM), BF16),
            pltpu.VMEM((2, TP, PART, HEAD_DIM), BF16),
            pltpu.VMEM((2, TP, PART, HEAD_DIM), BF16),
            pltpu.VMEM((2, SPAN - 1, TOK, HEAD_DIM), BF16),
            pltpu.VMEM((2, SPAN - 1, TOK, HEAD_DIM), BF16),
            pltpu.VMEM((1, TOK), jnp.int32),
            sem((5,)),
            sem((8,)),
            sem((6,)),
            sem((6,)),
            sem((5, SPAN)),
            sem((5, SPAN)),
            sem((4, SPAN - 1)),
            sem((4, SPAN - 1)),
            sem((4,)),
            sem((4,)),
            sem((2,)),
            sem((2,)),
            pltpu.SemaphoreType.REGULAR,
        ],
        compiler_params=pltpu.CompilerParams(
            collective_id=0, has_side_effects=True, vmem_limit_bytes=62 * 1024 * 1024
        ),
    )(query_in, key_in, value_in, grad_out, segments.reshape(1, TOK))
    return pl.pallas_call(
        deliver,
        out_shape=outs,
        in_specs=[hbm_spec] * 4,
        out_specs=(hbm_spec,) * 4,
        scratch_shapes=[pltpu.VMEM(out.shape, BF16) for out in outs] + [sem((4,)), sem((4,))],
        compiler_params=pltpu.CompilerParams(vmem_limit_bytes=62 * 1024 * 1024),
    )(*results)


def solution(mesh):
    split = P(("ctx", "tp"), None)
    return jax.shard_map(
        body,
        mesh=mesh,
        in_specs=(split, split, split, split, P("ctx")),
        out_specs=(split, split, split, split),
        check_vma=False,
    )
```
